256 devices in a mesh: dp: 8 (over z_hi, y), tensor: 8 (over z_lo, core), section: 4 (over x).
Axes of the slice: x: 4, y: 4, z: 8 (z_hi: 2, z_lo: 4; z = z_hi * 4 + z_lo), core: 2. Of those that a mesh axis runs over, the one named last changes fastest.
Arguments:
- tokens_in: bfloat16 [40960, 5120], P(('section', 'dp', 'tensor')), parts along dimension 0, may hold values from -4 to 4
- key_cot: bfloat16 [40960, 1024], P(('section', 'dp'), 'tensor'), parts along dimension 0, may hold values from -3 to 3, as said below
- row_mask: int32 [40960], P(('section', 'dp', 'tensor')), parts along dimension 0, may hold values 0 or 1
- w_key: bfloat16 [20480, 1024], P('section', 'tensor'), parts along dimension 0, may hold values from -0.078125 to 0.078125
- momentum: bfloat16 [8, 20480, 1024], P('dp', 'section', 'tensor'), parts along dimension 1, may hold values from -4 to 4
Outputs:
- input_grad: bfloat16 [40960, 5120], P(('section', 'dp', 'tensor')), parts along dimension 0
- new_momentum: bfloat16 [8, 20480, 1024], P('dp', 'section', 'tensor'), parts along dimension 1
- rollout_weight: bfloat16 [8, 20480, 256], P('tensor', 'section'), parts along dimension 1
The draws below stay inside these ranges and needn't reach their ends.
There are 4 independent parts, one for each index of `section`. The reference program is written for one: setup_inputs(seed, part) draws one part's arguments, and reference() takes and returns one part's arrays. A program takes and returns all parts, laid end to end along the dimension named above; each array names one. Nothing has to cross between parts.
Inputs may be any that keep to these rules, and one draw needn't show every extreme that they name: `key_cot`: every entry is a multiple of 0.125.
All inputs are finite; a program needn't handle non-finite values. No bound on the sum of `row_mask` on one device may be relied on, other than what follows from the above.
Results may differ from the reference program's by a relative error of at most 0.017.
Values may be sent and summed in bfloat16 or wider, within the bound.
No kernel may reach another device: no remote copies, remote signals or barrier semaphores. Data moves between devices by JAX's collectives and lax.ppermute only.
A program may use at most 128 MiB of HBM per device.

```python
import jax
import jax.numpy as jnp
from jax import lax

D = 5120
KV = 1024
SEQ_ROWS = 1280
ROWS = 10240
N_DP = 8
N_TENSOR = 8


def eighths(key, shape, reach):
    uniform_part = jax.random.uniform(key, shape, jnp.float32)
    return (jnp.floor(uniform_part * (2.0 * reach + 1.0)) - reach) / 8.0


def on_grid(values, quantum):
    stored = lax.optimization_barrier(values.astype(jnp.bfloat16)).astype(jnp.float32)
    return (jnp.floor(stored / quantum) * quantum).astype(jnp.bfloat16)


def draw_tokens_in(key, part):
    key = jax.random.fold_in(key, 11)
    longer = max(0, (SEQ_ROWS - 1).bit_length() - 10)
    quantum = 2.0 ** ((longer + 1) // 2 - 11)
    values = jnp.clip(jax.random.normal(key, (ROWS, D), jnp.float32), -4.0, 4.0)
    return on_grid(values, quantum)


def draw_key_cot(key, part):
    key = jax.random.fold_in(key, 23)
    values = eighths(key, (ROWS, KV), 16.0)
    return values.astype(jnp.bfloat16)


def plant(array, rng, smallest, top_value):
    spot = [jax.random.randint(jax.random.fold_in(rng, axis), (), 0, length) for axis, length in enumerate(array.shape)]
    widest = array.shape.index(max(array.shape))
    next_to = spot[:widest] + [(spot[widest] + 1) % array.shape[widest]] + spot[widest + 1:]
    return array.at[tuple(spot)].set(smallest).at[tuple(next_to)].set(top_value)


def shard_levels(key, dims, pieces, least, largest):
    def one(dim, blocks):
        draws = jax.random.uniform(jax.random.fold_in(jax.random.fold_in(key, 6), dim), (blocks,), jnp.float32, least / len(pieces), largest / len(pieces))
        return jnp.repeat(jnp.exp(draws), dims[dim] // blocks).reshape((-1,) + (1,) * (len(dims) - dim - 1))

    loudness = one(*pieces[0])
    for cut in pieces[1:]:
        loudness = loudness * one(*cut)
    return loudness


def noise(key, shape, spread, limit, shards=(), kind=jnp.bfloat16):
    entries = spread * jax.random.normal(key, shape, jnp.float32)
    if shards:
        entries = entries * shard_levels(key, shape, shards, -0.22, 0.18)
    return jnp.clip(entries, -limit, limit).astype(kind)


def setup_inputs(seed: int = 0, part: int = 0) -> dict:
    streams_of = jax.random.split(jax.random.key(seed), 6)
    part_keys = jax.random.split(jax.random.fold_in(streams_of[5], part), 6)
    tokens_in = draw_tokens_in(jax.random.fold_in(jax.random.fold_in(streams_of[5], part), 71), part)
    key_cot = draw_key_cot(jax.random.fold_in(jax.random.fold_in(streams_of[5], part), 71), part)
    row_mask = plant((jax.random.randint(part_keys[2], (ROWS,), 0, 4) < 3).astype(jnp.int32), jax.random.fold_in(part_keys[2], 1), 0, 1)
    w_key = noise(part_keys[3], (D, KV), D ** -0.5, 0.078125, ((1, 8),))
    momentum = noise(part_keys[4], (N_DP, D, KV), 0.5, 4.0, ((0, 8), (2, 8)))
    return {"tokens_in": tokens_in, "key_cot": key_cot, "row_mask": row_mask, "w_key": w_key, "momentum": momentum}


beta_slow = 0.99
beta_vote = 0.9
step_rate = 0.02


def reference(tokens_in, key_cot, row_mask, w_key, momentum):
    mask_half = row_mask.astype(jnp.bfloat16)[:, None]
    masked_cot = key_cot * mask_half

    def worker(worker_id):
        offset = worker_id * SEQ_ROWS
        token_block = lax.dynamic_slice_in_dim(tokens_in, offset, SEQ_ROWS, 0)
        cot_block = lax.dynamic_slice_in_dim(masked_cot, offset, SEQ_ROWS, 0)
        return lax.dot_general(token_block, cot_block, (((0,), (0,)), ((), ())), preferred_element_type=jnp.float32)

    key_grad = lax.map(worker, jnp.arange(N_DP, dtype=jnp.int32))
    prior = momentum.astype(jnp.float32)
    new_momentum = (beta_slow * prior + (1.0 - beta_slow) * key_grad).astype(jnp.bfloat16)
    interp = beta_vote * prior + (1.0 - beta_vote) * key_grad
    vote_count = jnp.sum((interp > 0).astype(jnp.int32), axis=0, dtype=jnp.int32)
    direction = jnp.sign((2 * vote_count - N_DP).astype(jnp.float32))
    updated = (w_key.astype(jnp.float32) - step_rate * direction).astype(jnp.bfloat16)
    blocks = updated.reshape(D, 4, KV // 4).transpose(1, 0, 2)
    rollout_weight = jnp.repeat(blocks, N_TENSOR // 4, axis=0)
    head_width = KV // N_TENSOR

    def head_group(running, group_id):
        cot_cols = lax.dynamic_slice_in_dim(key_cot, group_id * head_width, head_width, 1)
        weight_cols = lax.dynamic_slice_in_dim(w_key, group_id * head_width, head_width, 1)
        partial_term = lax.dot_general(cot_cols, weight_cols, (((1,), (1,)), ((), ())), preferred_element_type=jnp.float32).astype(jnp.bfloat16)
        return running + partial_term.astype(jnp.float32), None

    summed, _ = lax.scan(head_group, jnp.zeros((ROWS, D), jnp.float32), jnp.arange(N_TENSOR, dtype=jnp.int32))
    input_grad = (summed * row_mask.astype(jnp.float32)[:, None]).astype(jnp.bfloat16)
    return (input_grad, new_momentum, rollout_weight)
```

```python
import jax
import jax.numpy as jnp
from jax import lax
from jax.experimental import pallas as pl
from jax.experimental.pallas import tpu as pltpu
from jax.sharding import PartitionSpec as P

beta_slow = 0.99
beta_vote = 0.9
step_rate = 0.02

AXES = ("dp", "tensor")
HI, YS, LINE, CORES = 2, 4, 4, 2
WIDTH = 512
VMEM = 48 * 1024 * 1024


def permute(array, place):
    pairs = []
    for hi in range(HI):
        for y in range(YS):
            for c in range(LINE):
                for k in range(CORES):
                    to = place(hi, y, c, k)
                    if to is not None:
                        h2, y2, c2, k2 = to
                        source = ((hi * YS + y) * LINE + c) * CORES + k
                        target = ((h2 % HI * YS + y2 % YS) * LINE + c2) * CORES + k2
                        pairs.append((source, target))
    return lax.ppermute(array, AXES, pairs)


def core_swap(array):
    return permute(array, lambda h, y, c, k: (h, y, c, 1 - k))


def along_y(array, step):
    return permute(array, lambda h, y, c, k: (h, y - step, c, k))


def along_z(array, step):
    def place(h, y, c, k):
        z = (h * LINE + c - step) % (HI * LINE)
        return z // LINE, y, z % LINE, k

    return permute(array, place)


def opposite_heads(array):
    def place(h, y, c, k):
        z = (h * LINE + c + (2 if c >= 2 else -2)) % (HI * LINE)
        return z // LINE, y, z % LINE, k

    return permute(array, place)


def inward(array):
    return permute(array, lambda h, y, c, k: (h, y, c ^ 1, k) if c in (0, 3) else None)


def outward(array, flip=0):
    return permute(array, lambda h, y, c, k: (h ^ flip, y, c ^ 1, k) if c in (1, 2) else None)


def across(array):
    return permute(array, lambda h, y, c, k: (h, y, 3 - c, k) if c in (1, 2) else None)


def inner_flip(array):
    return permute(array, lambda h, y, c, k: (h ^ 1, y, c, k) if c in (1, 2) else None)


def params():
    return pltpu.CompilerParams(vmem_limit_bytes=VMEM)


def momentum_kernel(*refs):
    tokens = refs[:8]
    cot, prior_own, prior_side, new_own, new_side, words_own, words_side = refs[8:]
    rows = jnp.concatenate([ref[...] for ref in tokens], 0)
    grad = lax.dot_general(
        cot[...], rows, (((1,), (0,)), ((), ())), preferred_element_type=jnp.float32
    ).T
    for i, (prior, new, words) in enumerate(
        ((prior_own, new_own, words_own), (prior_side, new_side, words_side))
    ):
        part = grad[:, i * 128 : (i + 1) * 128]
        before = prior[...].astype(jnp.float32)
        new[...] = (beta_slow * before + (1.0 - beta_slow) * part).astype(jnp.bfloat16)
        positive = (beta_vote * before + (1.0 - beta_vote) * part > 0).astype(jnp.int32)
        step = WIDTH // 32
        packed = positive[:step]
        for bit in range(1, 32):
            packed = packed | (positive[bit * step : (bit + 1) * step] << bit)
        words[...] = packed


def momentum_step(tokens, cot, prior_own, prior_side, start, size):
    first = start // WIDTH
    token_specs = [
        pl.BlockSpec((160, WIDTH), (lambda i: (0, i + first)) if whole else (lambda i: (0, i)))
        for _, whole in tokens
    ]
    prior_spec = pl.BlockSpec((WIDTH, 128), lambda i: (i + first, 0))
    grad_spec = pl.BlockSpec((WIDTH, 128), lambda i: (i, 0))
    word_spec = pl.BlockSpec((WIDTH // 32, 128), lambda i: (i, 0))
    return pl.pallas_call(
        momentum_kernel,
        grid=(size // WIDTH,),
        in_specs=token_specs
        + [pl.BlockSpec((256, 1280), lambda i: (0, 0)), prior_spec, prior_spec],
        out_specs=[grad_spec, grad_spec, word_spec, word_spec],
        out_shape=[jax.ShapeDtypeStruct((size, 128), jnp.bfloat16)] * 2
        + [jax.ShapeDtypeStruct((size // 32, 128), jnp.int32)] * 2,
        compiler_params=params(),
        cost_estimate=pl.CostEstimate(
            flops=2 * size * 1280 * 256, bytes_accessed=size * 1280 * 2 + size * 1024, transcendentals=0
        ),
        name="momentum_step",
    )(*[array for array, _ in tokens], cot, prior_own, prior_side)


def majority(words):
    def half(a, b):
        return a ^ b, a & b

    def full(a, b, c):
        x = a ^ b
        return x ^ c, (a & b) | (x & c)

    s0, c0 = full(words[0], words[1], words[2])
    s1, c1 = full(words[3], words[4], words[5])
    s2, c2 = half(words[6], words[7])
    ones, c3 = full(s0, s1, s2)
    t0, d0 = full(c0, c1, c2)
    twos, d1 = half(t0, c3)
    fours, eights = half(d0, d1)
    more = eights | (fours & (ones | twos))
    fewer = ~(eights | fours)
    return more, fewer


def vote_kernel(core, words_own, words_other, w_own, w_other, out):
    is_low = core[0] == 0
    step = WIDTH // 32
    updated = []
    for words, weights in ((words_own, w_own), (words_other, w_other)):
        more, fewer = majority([words[i] for i in range(8)])
        direction = jnp.concatenate(
            [((more >> bit) & 1) - ((fewer >> bit) & 1) for bit in range(32)], 0
        ).astype(jnp.float32)
        updated.append((weights[...].astype(jnp.float32) - step_rate * direction).astype(jnp.bfloat16))
    out[:, :128] = jnp.where(is_low, updated[0], updated[1])
    out[:, 128:] = jnp.where(is_low, updated[1], updated[0])


def vote_step(core, words_own, words_other, w_own, w_other):
    features = w_own.shape[0]
    word_spec = pl.BlockSpec((8, WIDTH // 32, 128), lambda i, core: (0, i, 0))
    weight_spec = pl.BlockSpec((WIDTH, 128), lambda i, core: (i, 0))
    return pl.pallas_call(
        vote_kernel,
        grid_spec=pltpu.PrefetchScalarGridSpec(
            num_scalar_prefetch=1,
            grid=(features // WIDTH,),
            in_specs=[word_spec, word_spec, weight_spec, weight_spec],
            out_specs=pl.BlockSpec((WIDTH, 256), lambda i, core: (i, 0)),
        ),
        out_shape=jax.ShapeDtypeStruct((features, 256), jnp.bfloat16),
        compiler_params=params(),
        cost_estimate=pl.CostEstimate(flops=features * 256 * 8, bytes_accessed=features * 1280, transcendentals=0),
        name="vote_step",
    )(core, words_own, words_other, w_own, w_other)


def partial_kernel(place, cot, weights, out):
    out[...] = lax.dot_general(
        cot[...], weights[0], (((1,), (1,)), ((), ())), preferred_element_type=jnp.float32
    ).astype(jnp.bfloat16)


def total_kernel(place, cot, weights, other, mask, out):
    total = lax.dot_general(
        cot[...], weights[0], (((1,), (1,)), ((), ())), preferred_element_type=jnp.float32
    ) + other[...].astype(jnp.float32)
    out[...] = (total * mask[...]).astype(jnp.bfloat16)


def input_step(place, cot, weights, other=None, mask=None):
    blocks, width, depth = weights.shape
    rows = cot.shape[0]
    out_spec = pl.BlockSpec((rows, width), lambda i, place: (0, place[i]))
    in_specs = [
        pl.BlockSpec((rows, depth), lambda i, place: (0, 0)),
        pl.BlockSpec((1, width, depth), lambda i, place: (i, 0, 0)),
    ]
    args = [cot, weights]
    if other is not None:
        in_specs += [out_spec, pl.BlockSpec((rows, 1), lambda i, place: (0, 0))]
        args += [other, mask]
    return pl.pallas_call(
        partial_kernel if other is None else total_kernel,
        grid_spec=pltpu.PrefetchScalarGridSpec(
            num_scalar_prefetch=1, grid=(blocks,), in_specs=in_specs, out_specs=out_spec
        ),
        out_shape=jax.ShapeDtypeStruct((rows, blocks * width), jnp.bfloat16),
        compiler_params=params(),
        cost_estimate=pl.CostEstimate(
            flops=2 * rows * depth * blocks * width,
            bytes_accessed=2 * (depth + 2 * rows) * blocks * width,
            transcendentals=0,
        ),
        name="input_step",
    )(place, *args)


def after(array, *others):
    return lax.optimization_barrier((array, *others))[0]


def per_device(tokens_in, key_cot, row_mask, w_key, momentum):
    position = lax.axis_index("tensor")
    chip, core = position // CORES, position % CORES
    y = lax.axis_index("dp") % YS
    inner = (chip == 1) | (chip == 2)
    features = w_key.shape[0]
    share = tokens_in.shape[0]
    quarter = features // YS
    cut = 2560

    tokens = jnp.where(row_mask[:, None] != 0, tokens_in, jnp.zeros_like(tokens_in))
    low, high = tokens[:, :cut], tokens[:, cut:]
    prior = momentum[0]

    def cot_rows(array, of_chip, of_core):
        return lax.dynamic_slice(array, ((of_chip * CORES + of_core) * share, 0), (share, 128))

    w_part = lax.dynamic_slice(w_key, (y * quarter, 0), (quarter, 128))
    w_up, w_down = along_z(w_part, 1), along_z(w_part, -1)
    w_far = opposite_heads(w_part)
    cot_pieces = []
    for step in (0, 1, 3, 2):
        rows = lax.dynamic_slice(
            key_cot, ((chip - step) % LINE * CORES * share, 0), (CORES * share, 128)
        )
        if step:
            rows = permute(rows, lambda h, y, c, k, step=step: (h, y, (c - step) % LINE, k))
        cot_pieces.append(rows)
    cot_mine = jnp.concatenate(cot_pieces, 1)
    cot_side = inward(key_cot)
    w_other = core_swap(w_key)

    from_across = across(tokens)
    from_side = [inward(low), inward(high)]
    w_here = jnp.concatenate([w_part, w_up, w_down, w_far], 1)
    w_next, w_before = along_y(w_here, 1), along_y(w_here, -1)
    w_next_far = along_y(w_next[: quarter // 2], 1)
    w_before_far = along_y(w_before[quarter // 2 :], -1)
    weights = jnp.concatenate([w_here, w_next, w_before, w_next_far, w_before_far], 0).reshape(
        8, quarter // 2, 512
    )
    from_far = [across(part) for part in from_side]
    prior_side = inward(prior)

    own_swapped = core_swap(tokens)
    across_swapped = core_swap(from_across)
    side_swapped = [core_swap(part) for part in from_side]
    far_swapped = [core_swap(part) for part in from_far]

    both = jnp.concatenate([key_cot, cot_side], 1)
    order = [chip, chip ^ 1, 3 - chip, (3 - chip) ^ 1]
    cot_all = jnp.concatenate(
        [
            lax.dynamic_slice(both, ((of_chip * CORES + of_core) * share, 0), (share, 256))
            for of_chip in order
            for of_core in (core, 1 - core)
        ],
        0,
    ).T
    new_own, new_side, words_own, words_side = [], [], [], []
    for i, (start, size) in enumerate(((0, cut), (cut, features - cut))):
        parts = [
            (tokens, True),
            (own_swapped, True),
            (from_side[i], False),
            (side_swapped[i], False),
            (from_across, True),
            (across_swapped, True),
            (from_far[i], False),
            (far_swapped[i], False),
        ]
        results = momentum_step(parts, cot_all, prior, prior_side, start, size)
        new_own.append(results[0])
        new_side.append(outward(results[1]))
        words_own.append(results[2])
        words_side.append(results[3])
    new_momentum = jnp.where(
        inner, jnp.concatenate(new_own, 0), jnp.concatenate(new_side, 0)
    )[None]

    mine, side = jnp.concatenate(words_own, 0), jnp.concatenate(words_side, 0)
    mine_flip = inner_flip(mine)
    side_here = outward(side)
    side_flip = outward(side, 1)
    pair = jnp.where(inner, jnp.stack([mine, mine_flip]), jnp.stack([side_here, side_flip]))
    words = jnp.concatenate([pair, along_y(pair, 1), along_y(pair, -1), along_y(pair, 2)], 0)
    words_other = core_swap(words)
    rollout_weight = vote_step(core[None], words, words_other, w_key, w_other)[None]

    quarters = jnp.stack([y, (y + 1) % YS, (y + 3) % YS, (y + 2) % YS])
    place = (quarters[:, None] * 2 + jnp.arange(2)[None, :]).reshape(8).astype(jnp.int32)
    theirs = lax.dynamic_slice(cot_mine, ((1 - core) * share, 0), (share, 512))
    ours = lax.dynamic_slice(cot_mine, (core * share, 0), (share, 512))
    other = core_swap(input_step(place, theirs, weights))
    input_grad = input_step(place, ours, weights, other, row_mask.astype(jnp.float32)[:, None])
    return (input_grad, new_momentum, rollout_weight)


def solution(mesh):
    return jax.shard_map(
        per_device,
        mesh=mesh,
        in_specs=(
            P(("section", "dp", "tensor"), None),
            P(("section", "dp"), "tensor"),
            P(("section", "dp", "tensor")),
            P("section", "tensor"),
            P("dp", "section", "tensor"),
        ),
        out_specs=(
            P(("section", "dp", "tensor"), None),
            P("dp", "section", "tensor"),
            P("tensor", "section", None),
        ),
        check_vma=False,
    )
```

```python
import jax
import jax.numpy as jnp
from jax import lax
from jax.experimental import pallas as pl
from jax.experimental.pallas import tpu as pltpu
from jax.sharding import PartitionSpec as P

beta_slow = 0.99
beta_vote = 0.9
step_rate = 0.02

AXES = ("dp", "tensor")
HI, YS, LINE, CORES = 2, 4, 4, 2
WIDTH = 1280
CUT = 2560
VMEM = 48 * 1024 * 1024


def permute(array, place):
    pairs = []
    for hi in range(HI):
        for y in range(YS):
            for c in range(LINE):
                for k in range(CORES):
                    to = place(hi, y, c, k)
                    if to is not None:
                        h2, y2, c2, k2 = to
                        source = ((hi * YS + y) * LINE + c) * CORES + k
                        target = ((h2 % HI * YS + y2 % YS) * LINE + c2) * CORES + k2
                        pairs.append((source, target))
    return lax.ppermute(array, AXES, pairs)


def core_swap(array):
    return permute(array, lambda h, y, c, k: (h, y, c, 1 - k))


def along_y(array, step):
    return permute(array, lambda h, y, c, k: (h, y - step, c, k))


def in_pair(array):
    return permute(array, lambda h, y, c, k: (h, y, c ^ 1, k))


def out_of_pair(array):
    def place(h, y, c, k):
        z = (h * LINE + c + (1 if c % 2 else -1)) % (HI * LINE)
        return z // LINE, y, z % LINE, k

    return permute(array, place)


def along_z(array, step):
    def place(h, y, c, k):
        z = (h * LINE + c - step) % (HI * LINE)
        return z // LINE, y, z % LINE, k

    return permute(array, place)


def inward(array):
    return permute(array, lambda h, y, c, k: (h, y, c ^ 1, k) if c in (0, 3) else None)


def outward(array, flip=0):
    return permute(array, lambda h, y, c, k: (h ^ flip, y, c ^ 1, k) if c in (1, 2) else None)


def across(array):
    return permute(array, lambda h, y, c, k: (h, y, 3 - c, k) if c in (1, 2) else None)


def inner_flip(array):
    return permute(array, lambda h, y, c, k: (h ^ 1, y, c, k) if c in (1, 2) else None)


def params():
    return pltpu.CompilerParams(vmem_limit_bytes=VMEM)


def cot_rows(place, first, count, cot_own, cot_side):
    share = cot_own.shape[0] // (LINE * CORES)
    blocks = [pl.ds(pl.multiple_of(place[first + i] * share, share), share) for i in range(count)]
    return jnp.concatenate(
        [jnp.concatenate([ref[block, :] for block in blocks], 0) for ref in (cot_own, cot_side)], 1
    )


def multiply(tokens, cot):
    rows = jnp.concatenate([ref[...] for ref in tokens], 0)
    return lax.dot_general(rows, cot, (((0,), (0,)), ((), ())), preferred_element_type=jnp.float32)


def gather_kernel(place, *refs):
    tokens, cot_own, cot_side, out = refs[:-3], refs[-3], refs[-2], refs[-1]
    out[...] = multiply(tokens, cot_rows(place, 0, len(tokens), cot_own, cot_side))


def gather_step(place, tokens, cot_own, cot_side, start, size):
    share, rows = tokens[0][0].shape[0], cot_own.shape[0]
    return pl.pallas_call(
        gather_kernel,
        grid_spec=pltpu.PrefetchScalarGridSpec(
            num_scalar_prefetch=1,
            grid=(size // WIDTH,),
            in_specs=[
                pl.BlockSpec((share, WIDTH), lambda i, place, skip=first // WIDTH: (0, i + skip))
                for _, first in tokens
            ]
            + [
                pl.BlockSpec((rows, 128), lambda i, place: (0, 0)),
                pl.BlockSpec((rows, 128), lambda i, place: (cot_side[1], 0)),
            ],
            out_specs=pl.BlockSpec((WIDTH, 256), lambda i, place: (i, 0)),
        ),
        out_shape=jax.ShapeDtypeStruct((size, 256), jnp.float32),
        compiler_params=params(),
        cost_estimate=pl.CostEstimate(
            flops=2 * size * 960 * 256, bytes_accessed=size * 2944, transcendentals=0
        ),
        name="gather_step",
    )(place, *[array for array, _ in tokens], cot_own, cot_side[0])


def momentum_kernel(place, *refs):
    first, second, cot_own, cot_side, early, prior_own, prior_side = refs[:7]
    new_own, new_side, words_own, words_side = refs[-4:]
    grad = early[...] + multiply((first, second), cot_rows(place, 6, 2, cot_own, cot_side))
    for i, (prior, new, words) in enumerate(
        ((prior_own, new_own, words_own), (prior_side, new_side, words_side))
    ):
        part = grad[:, i * 128 : (i + 1) * 128]
        before = prior[...].astype(jnp.float32)
        new[...] = (beta_slow * before + (1.0 - beta_slow) * part).astype(jnp.bfloat16)
        positive = (beta_vote * before + (1.0 - beta_vote) * part > 0).astype(jnp.int32)
        step = WIDTH // 32
        packed = positive[:step]
        for bit in range(1, 32):
            packed = packed | (positive[bit * step : (bit + 1) * step] << bit)
        words[...] = packed


def momentum_step(place, first, second, cot_own, cot_side, early, prior_own, prior_side, start, buffers):
    share, size = first.shape
    rows = cot_own.shape[0]
    features = prior_own.shape[0]
    skip = start // WIDTH
    here = lambda i, place: (i, 0)
    there = lambda i, place: (i + skip, 0)
    token_spec = pl.BlockSpec((share, WIDTH), lambda i, place: (0, i))
    word_spec = pl.BlockSpec((WIDTH // 32, 128), there)
    word_shape = jax.ShapeDtypeStruct((features // 32, 128), jnp.int32)
    return pl.pallas_call(
        momentum_kernel,
        grid_spec=pltpu.PrefetchScalarGridSpec(
            num_scalar_prefetch=1,
            grid=(size // WIDTH,),
            in_specs=[
                token_spec,
                token_spec,
                pl.BlockSpec((rows, 128), lambda i, place: (0, 0)),
                pl.BlockSpec((rows, 128), lambda i, place: (cot_side[1], 0)),
                pl.BlockSpec((WIDTH, 256), here),
                pl.BlockSpec((WIDTH, 128), there),
                pl.BlockSpec((WIDTH, 128), here),
            ]
            + [pl.BlockSpec(memory_space=pl.ANY)] * len(buffers),
            out_specs=[
                pl.BlockSpec((WIDTH, 128), there),
                pl.BlockSpec((WIDTH, 128), here),
                word_spec,
                word_spec,
            ],
        ),
        out_shape=[
            jax.ShapeDtypeStruct((features, 128), jnp.bfloat16),
            jax.ShapeDtypeStruct((size, 128), jnp.bfloat16),
            word_shape,
            word_shape,
        ],
        input_output_aliases={8: 0, 9: 2, 10: 3} if buffers else {},
        compiler_params=params(),
        cost_estimate=pl.CostEstimate(
            flops=2 * size * 320 * 256, bytes_accessed=size * 2688, transcendentals=0
        ),
        name="momentum_step",
    )(place, first, second, cot_own, cot_side[0], early, prior_own, prior_side, *buffers)


def majority(words):
    def half(a, b):
        return a ^ b, a & b

    def full(a, b, c):
        x = a ^ b
        return x ^ c, (a & b) | (x & c)

    s0, c0 = full(words[0], words[1], words[2])
    s1, c1 = full(words[3], words[4], words[5])
    s2, c2 = half(words[6], words[7])
    ones, c3 = full(s0, s1, s2)
    t0, d0 = full(c0, c1, c2)
    twos, d1 = half(t0, c3)
    fours, eights = half(d0, d1)
    more = eights | (fours & (ones | twos))
    fewer = ~(eights | fours)
    return more, fewer


def vote_kernel(core, words_own, words_other, w_own, w_other, out):
    is_low = core[0] == 0
    step = WIDTH // 32
    for block in range(out.shape[0] // WIDTH):
        rows = slice(block * WIDTH, (block + 1) * WIDTH)
        updated = []
        for words, weights in ((words_own, w_own), (words_other, w_other)):
            more, fewer = majority([words[i, block * step : (block + 1) * step] for i in range(8)])
            direction = jnp.concatenate(
                [((more >> bit) & 1) - ((fewer >> bit) & 1) for bit in range(32)], 0
            ).astype(jnp.float32)
            updated.append(
                (weights[rows, :].astype(jnp.float32) - step_rate * direction).astype(jnp.bfloat16)
            )
        out[rows, :128] = jnp.where(is_low, updated[0], updated[1])
        out[rows, 128:] = jnp.where(is_low, updated[1], updated[0])


def vote_step(core, words_own, words_other, w_own, w_other):
    features = w_own.shape[0]
    size = 2 * WIDTH
    word_spec = pl.BlockSpec((8, size // 32, 128), lambda i, core: (0, i, 0))
    weight_spec = pl.BlockSpec((size, 128), lambda i, core: (i, 0))
    return pl.pallas_call(
        vote_kernel,
        grid_spec=pltpu.PrefetchScalarGridSpec(
            num_scalar_prefetch=1,
            grid=(features // size,),
            in_specs=[word_spec, word_spec, weight_spec, weight_spec],
            out_specs=pl.BlockSpec((size, 256), lambda i, core: (i, 0)),
        ),
        out_shape=jax.ShapeDtypeStruct((features, 256), jnp.bfloat16),
        compiler_params=params(),
        cost_estimate=pl.CostEstimate(flops=features * 256 * 8, bytes_accessed=features * 1280, transcendentals=0),
        name="vote_step",
    )(core, words_own, words_other, w_own, w_other)


def input_kernel(cot, w_own, w_rest, ours, theirs):
    weights = jnp.concatenate([w_own[...], w_rest[...]], 1)
    total = lax.dot_general(
        cot[...], weights, (((1,), (1,)), ((), ())), preferred_element_type=jnp.float32
    ).astype(jnp.bfloat16)
    rows = ours.shape[0]
    ours[...] = total[:rows]
    theirs[...] = total[rows:]


def input_step(cot, w_own, w_rest):
    rows, depth = cot.shape
    features = w_own.shape[0]
    width = 2 * WIDTH
    out_spec = pl.BlockSpec((rows // 2, width), lambda i: (0, i))
    return pl.pallas_call(
        input_kernel,
        grid=(features // width,),
        in_specs=[pl.BlockSpec((rows, depth), lambda i: (0, 0))]
        + [pl.BlockSpec((width, w.shape[1]), lambda i: (i, 0)) for w in (w_own, w_rest)],
        out_specs=[out_spec] * 2,
        out_shape=[jax.ShapeDtypeStruct((rows // 2, features), jnp.bfloat16)] * 2,
        compiler_params=params(),
        cost_estimate=pl.CostEstimate(
            flops=2 * rows * depth * features, bytes_accessed=2 * (depth + rows) * features, transcendentals=0
        ),
        name="input_step",
    )(cot, w_own, w_rest)


def after(arrays, *others):
    return lax.optimization_barrier((arrays, *others))[0]


def per_device(tokens_in, key_cot, row_mask, w_key, momentum):
    position = lax.axis_index("tensor")
    chip, core = position // CORES, position % CORES
    y = lax.axis_index("dp") % YS
    inner = (chip == 1) | (chip == 2)
    features = w_key.shape[0]
    share = tokens_in.shape[0]
    quarter = features // YS
    cut = CUT
    prior = momentum[0]
    place = jnp.stack(
        [
            of_chip * CORES + of_core
            for of_chip in (chip, chip ^ 1, chip ^ 3, chip ^ 2)
            for of_core in (core, 1 - core)
        ]
    ).astype(jnp.int32)

    w_part = lax.dynamic_slice(w_key, (y * quarter, 0), (quarter, 128))
    w_rest = [
        in_pair(w_part),
        out_of_pair(w_part),
        along_z(w_part[: quarter // 2], 2),
        along_z(w_part[quarter // 2 :], -2),
    ]
    tokens = jnp.where(row_mask[:, None] != 0, tokens_in, jnp.zeros_like(tokens_in))
    tokens, w_rest = lax.optimization_barrier((tokens, w_rest))
    w_rest = lax.all_gather(
        jnp.concatenate([w_rest[0], w_rest[1], jnp.concatenate(w_rest[2:], 0)], 1),
        "dp",
        axis=0,
        tiled=True,
        axis_index_groups=[[h * YS + y for y in range(YS)] for h in range(HI)],
    )

    near, side, own_swapped = across(tokens), inward(tokens), core_swap(tokens)
    cot_pieces = []
    for step in (0, 1, 3, 2):
        rows = lax.dynamic_slice(key_cot, ((chip ^ step) * CORES * share, 0), (CORES * share, 128))
        if step:
            rows = permute(rows, lambda h, y, c, k, step=step: (h, y, c ^ step, k))
        cot_pieces.append(rows)
    lend = jnp.concatenate([prior[:cut], key_cot], 0)
    near, side, own_swapped, cot_pieces, lend = lax.optimization_barrier(
        (near, side, own_swapped, cot_pieces, lend)
    )

    far = across(side[:, :cut])
    lent = inward(lend)
    near_swapped, side_swapped, w_other = core_swap(near), core_swap(side), core_swap(w_key)
    far, lent, near_swapped, side_swapped, w_other = lax.optimization_barrier(
        (far, lent, near_swapped, side_swapped, w_other)
    )

    far_late = across(side[:, cut:])
    lent_late = inward(prior[cut:])
    cot_side = (lent, cut // key_cot.shape[0])
    arrays = (tokens, own_swapped, side, side_swapped, near, near_swapped)

    def early(start):
        return gather_step(place, [(array, start) for array in arrays], key_cot, cot_side, start, cut)

    new_own, new_side, words, side_words = momentum_step(
        place, far, core_swap(far), key_cot, cot_side, early(0), prior, lent, 0, []
    )
    returned = [outward(new_side)]
    summed, far_late, lent_late, new_own, words, side_words, cot_pieces = lax.optimization_barrier(
        (early(cut), far_late, lent_late, new_own, words, side_words, cot_pieces)
    )

    new_own, new_side, words, side_words = momentum_step(
        place, far_late, core_swap(far_late), key_cot, cot_side, summed, prior, lent_late, cut,
        [new_own, words, side_words],
    )
    words, cot_pieces = lax.optimization_barrier((words, cot_pieces))
    words_flip = inner_flip(words)
    side_here, side_flip = outward(side_words), outward(side_words, 1)
    cot_mine = jnp.concatenate(cot_pieces, 1)
    theirs = lax.dynamic_slice(cot_mine, ((1 - core) * share, 0), (share, 512))
    ours = lax.dynamic_slice(cot_mine, (core * share, 0), (share, 512))
    ours, theirs = input_step(jnp.concatenate([ours, theirs], 0), w_key, w_rest)
    words_flip, side_here, side_flip, returned[0], new_side, ours, theirs = lax.optimization_barrier(
        (words_flip, side_here, side_flip, returned[0], new_side, ours, theirs)
    )

    pair = jnp.where(inner, jnp.stack([words, words_flip]), jnp.stack([side_here, side_flip]))
    votes = jnp.concatenate([pair, along_y(pair, 1), along_y(pair, -1), along_y(pair, 2)], 0)
    returned.append(outward(new_side))
    total = ours.astype(jnp.float32) + core_swap(theirs).astype(jnp.float32)
    input_grad = (total * row_mask.astype(jnp.float32)[:, None]).astype(jnp.bfloat16)
    new_momentum = jnp.where(inner, new_own, jnp.concatenate(returned, 0))[None]
    votes_other, new_momentum, input_grad = after((core_swap(votes), new_momentum, input_grad))
    rollout_weight = vote_step(core[None], votes, votes_other, w_key, w_other)[None]
    return (input_grad, new_momentum, rollout_weight)


def solution(mesh):
    return jax.shard_map(
        per_device,
        mesh=mesh,
        in_specs=(
            P(("section", "dp", "tensor"), None),
            P(("section", "dp"), "tensor"),
            P(("section", "dp", "tensor")),
            P("section", "tensor"),
            P("dp", "section", "tensor"),
        ),
        out_specs=(
            P(("section", "dp", "tensor"), None),
            P("dp", "section", "tensor"),
            P("tensor", "section", None),
        ),
        check_vma=False,
    )
```

```python
import jax
import jax.numpy as jnp
from jax import lax
from jax.experimental import pallas as pl
from jax.experimental.pallas import tpu as pltpu
from jax.sharding import PartitionSpec as P

beta_slow = 0.99
beta_vote = 0.9
step_rate = 0.02

AXES = ("dp", "tensor")
HI, YS, LINE, CORES = 2, 4, 4, 2
WIDTH = 1024
CUT = 2048
COST = pl.CostEstimate(flops=2_000_000_000, bytes_accessed=10_000_000, transcendentals=0)
VMEM = 48 * 1024 * 1024


def permute(array, place):
    pairs = []
    for hi in range(HI):
        for y in range(YS):
            for c in range(LINE):
                for k in range(CORES):
                    to = place(hi, y, c, k)
                    if to is not None:
                        h2, y2, c2, k2 = to
                        source = ((hi * YS + y) * LINE + c) * CORES + k
                        target = ((h2 % HI * YS + y2 % YS) * LINE + c2) * CORES + k2
                        pairs.append((source, target))
    return lax.ppermute(array, AXES, pairs)


def core_swap(array):
    return permute(array, lambda h, y, c, k: (h, y, c, 1 - k))


def along_y(array, step):
    return permute(array, lambda h, y, c, k: (h, y - step, c, k))


def in_pair(array):
    return permute(array, lambda h, y, c, k: (h, y, c ^ 1, k))


def out_of_pair(array):
    def place(h, y, c, k):
        z = (h * LINE + c + (1 if c % 2 else -1)) % (HI * LINE)
        return z // LINE, y, z % LINE, k

    return permute(array, place)


def opposite_heads(array):
    def place(h, y, c, k):
        z = (h * LINE + c + (2 if c >= 2 else -2)) % (HI * LINE)
        return z // LINE, y, z % LINE, k

    return permute(array, place)


def inward(array):
    return permute(array, lambda h, y, c, k: (h, y, c ^ 1, k) if c in (0, 3) else None)


def outward(array):
    return permute(array, lambda h, y, c, k: (h, y, c ^ 1, k) if c in (1, 2) else None)


def across(array):
    return permute(array, lambda h, y, c, k: (h, y, 3 - c, k) if c in (1, 2) else None)


def z_flip(array):
    return permute(array, lambda h, y, c, k: (h ^ 1, y, c, k))


def params():
    return pltpu.CompilerParams(vmem_limit_bytes=VMEM)


def cot_rows(place, first, count, cot_own, cot_side):
    share = cot_own.shape[0] // (LINE * CORES)
    blocks = [pl.ds(pl.multiple_of(place[first + i] * share, share), share) for i in range(count)]
    return jnp.concatenate(
        [jnp.concatenate([ref[block, :] for block in blocks], 0) for ref in (cot_own, cot_side)], 1
    )


def multiply(tokens, cot):
    rows = jnp.concatenate([ref[...] for ref in tokens], 0)
    return lax.dot_general(rows, cot, (((0,), (0,)), ((), ())), preferred_element_type=jnp.float32)


def gather_kernel(place, *refs):
    tokens, cot_own, cot_side, out, cot = refs[:-4], refs[-4], refs[-3], refs[-2], refs[-1]

    @pl.when(pl.program_id(0) == 0)
    def _():
        cot[...] = cot_rows(place, 0, len(tokens), cot_own, cot_side)

    out[...] = multiply(tokens, cot[...])


def gather_step(place, tokens, cot_own, cot_side, start, size):
    share, rows = tokens[0][0].shape[0], cot_own.shape[0]
    return pl.pallas_call(
        gather_kernel,
        grid_spec=pltpu.PrefetchScalarGridSpec(
            num_scalar_prefetch=1,
            grid=(size // WIDTH,),
            in_specs=[
                pl.BlockSpec((share, WIDTH), lambda i, place, skip=first // WIDTH: (0, i + skip))
                for _, first in tokens
            ]
            + [
                pl.BlockSpec((rows, 128), lambda i, place: (0, 0)),
                pl.BlockSpec((rows, 128), lambda i, place: (cot_side[1], 0)),
            ],
            out_specs=pl.BlockSpec((WIDTH, 256), lambda i, place: (i, 0)),
            scratch_shapes=[pltpu.VMEM((len(tokens) * share, 256), jnp.bfloat16)],
        ),
        out_shape=jax.ShapeDtypeStruct((size, 256), jnp.float32),
        compiler_params=params(),
        cost_estimate=COST,
        name="gather_step",
    )(place, *[array for array, _ in tokens], cot_own, cot_side[0])


def momentum_kernel(place, *refs):
    first, second, cot_own, cot_side, early, prior_own, prior_side = refs[:7]
    new_own, new_side, words_own, words_side = refs[-4:]
    grad = early[...] + multiply((first, second), cot_rows(place, 6, 2, cot_own, cot_side))
    for i, (prior, new, words) in enumerate(
        ((prior_own, new_own, words_own), (prior_side, new_side, words_side))
    ):
        part = grad[:, i * 128 : (i + 1) * 128]
        before = prior[...].astype(jnp.float32)
        new[...] = (beta_slow * before + (1.0 - beta_slow) * part).astype(jnp.bfloat16)
        positive = (beta_vote * before + (1.0 - beta_vote) * part > 0).astype(jnp.int32)
        step = WIDTH // 32
        packed = positive[:step]
        for bit in range(1, 32):
            packed = packed | (positive[bit * step : (bit + 1) * step] << bit)
        words[...] = packed


def momentum_step(place, first, second, cot_own, cot_side, early, prior_own, prior_side, start, buffers):
    share, size = first.shape
    rows = cot_own.shape[0]
    features = prior_own.shape[0]
    skip = start // WIDTH
    here = lambda i, place: (i, 0)
    there = lambda i, place: (i + skip, 0)
    token_spec = pl.BlockSpec((share, WIDTH), lambda i, place: (0, i))
    word_spec = pl.BlockSpec((WIDTH // 32, 128), there)
    word_shape = jax.ShapeDtypeStruct((features // 32, 128), jnp.int32)
    return pl.pallas_call(
        momentum_kernel,
        grid_spec=pltpu.PrefetchScalarGridSpec(
            num_scalar_prefetch=1,
            grid=(size // WIDTH,),
            in_specs=[
                token_spec,
                token_spec,
                pl.BlockSpec((rows, 128), lambda i, place: (0, 0)),
                pl.BlockSpec((rows, 128), lambda i, place: (cot_side[1], 0)),
                pl.BlockSpec((WIDTH, 256), here),
                pl.BlockSpec((WIDTH, 128), there),
                pl.BlockSpec((WIDTH, 128), here),
            ]
            + [pl.BlockSpec(memory_space=pl.ANY)] * len(buffers),
            out_specs=[
                pl.BlockSpec((WIDTH, 128), there),
                pl.BlockSpec((WIDTH, 128), here),
                word_spec,
                word_spec,
            ],
        ),
        out_shape=[
            jax.ShapeDtypeStruct((features, 128), jnp.bfloat16),
            jax.ShapeDtypeStruct((size, 128), jnp.bfloat16),
            word_shape,
            word_shape,
        ],
        input_output_aliases={8: 0, 9: 2, 10: 3} if buffers else {},
        compiler_params=params(),
        cost_estimate=COST,
        name="momentum_step",
    )(place, first, second, cot_own, cot_side[0], early, prior_own, prior_side, *buffers)


def majority(words):
    def half(a, b):
        return a ^ b, a & b

    def full(a, b, c):
        x = a ^ b
        return x ^ c, (a & b) | (x & c)

    s0, c0 = full(words[0], words[1], words[2])
    s1, c1 = full(words[3], words[4], words[5])
    s2, c2 = half(words[6], words[7])
    ones, c3 = full(s0, s1, s2)
    t0, d0 = full(c0, c1, c2)
    twos, d1 = half(t0, c3)
    fours, eights = half(d0, d1)
    more = eights | (fours & (ones | twos))
    fewer = ~(eights | fours)
    return more, fewer


def choose_kernel(inner, own, returned, out):
    out[...] = jnp.where(inner[0] == 1, own[...], returned[...])


def choose_step(inner, own, returned, start):
    skip = start // WIDTH
    there = pl.BlockSpec((WIDTH, 128), lambda i, inner: (i + skip, 0))
    return pl.pallas_call(
        choose_kernel,
        grid_spec=pltpu.PrefetchScalarGridSpec(
            num_scalar_prefetch=1,
            grid=(returned.shape[0] // WIDTH,),
            in_specs=[there, pl.BlockSpec((WIDTH, 128), lambda i, inner: (i, 0))],
            out_specs=there,
        ),
        out_shape=jax.ShapeDtypeStruct(own.shape, own.dtype),
        input_output_aliases={1: 0},
        compiler_params=params(),
        cost_estimate=COST,
        name="choose_step",
    )(inner, own, returned)


def vote_kernel(core, *refs):
    words_own, words_other, (w_own, w_other, out) = refs[:4], refs[4:8], refs[8:]
    is_low = core[0] == 0
    step = WIDTH // 32
    for block in range(out.shape[0] // WIDTH):
        rows = slice(block * WIDTH, (block + 1) * WIDTH)
        updated = []
        for words, weights in ((words_own, w_own), (words_other, w_other)):
            more, fewer = majority(
                [ref[i, block * step : (block + 1) * step] for ref in words for i in range(2)]
            )
            direction = jnp.concatenate(
                [((more >> bit) & 1) - ((fewer >> bit) & 1) for bit in range(32)], 0
            ).astype(jnp.float32)
            updated.append(
                (weights[rows, :].astype(jnp.float32) - step_rate * direction).astype(jnp.bfloat16)
            )
        out[rows, :128] = jnp.where(is_low, updated[0], updated[1])
        out[rows, 128:] = jnp.where(is_low, updated[1], updated[0])


def vote_step(core, words_own, words_other, w_own, w_other):
    features = w_own.shape[0]
    size = WIDTH
    word_spec = pl.BlockSpec((2, size // 32, 128), lambda i, core: (0, i, 0))
    weight_spec = pl.BlockSpec((size, 128), lambda i, core: (i, 0))
    return pl.pallas_call(
        vote_kernel,
        grid_spec=pltpu.PrefetchScalarGridSpec(
            num_scalar_prefetch=1,
            grid=(features // size,),
            in_specs=[word_spec] * 8 + [weight_spec] * 2,
            out_specs=pl.BlockSpec((size, 256), lambda i, core: (i, 0)),
        ),
        out_shape=jax.ShapeDtypeStruct((features, 256), jnp.bfloat16),
        compiler_params=params(),
        cost_estimate=COST,
        name="vote_step",
    )(core, *words_own, *words_other, w_own, w_other)


def input_kernel(place, cot, w_own, here, following, before, far_low, far_high, ours, theirs):
    rows = ours.shape[0]

    def product(w_rest):
        weights = jnp.concatenate([w_own[...], w_rest], 1)
        total = lax.dot_general(
            cot[...], weights, (((1,), (1,)), ((), ())), preferred_element_type=jnp.float32
        ).astype(jnp.bfloat16)
        ours[...] = total[:rows]
        theirs[...] = total[rows:]

    i = pl.program_id(0)
    for at, ref in enumerate((here, following, before)):
        pl.when(i == at)(lambda ref=ref: product(ref[...]))
    pl.when(i == 3)(lambda: product(jnp.concatenate([far_low[...], far_high[...]], 0)))


def input_step(place, cot, w_own, w_rest):
    rows, depth = cot.shape
    features = w_own.shape[0]
    width = features // YS
    out_spec = pl.BlockSpec((rows // 2, width), lambda i, place: (0, place[i]))
    return pl.pallas_call(
        input_kernel,
        grid_spec=pltpu.PrefetchScalarGridSpec(
            num_scalar_prefetch=1,
            grid=(YS,),
            in_specs=[
                pl.BlockSpec((rows, depth), lambda i, place: (0, 0)),
                pl.BlockSpec((width, 128), lambda i, place: (place[i], 0)),
            ]
            + [pl.BlockSpec(w.shape, lambda i, place: (0, 0)) for w in w_rest],
            out_specs=[out_spec] * 2,
        ),
        out_shape=[jax.ShapeDtypeStruct((rows // 2, features), jnp.bfloat16)] * 2,
        compiler_params=params(),
        cost_estimate=pl.CostEstimate(
            flops=2 * rows * depth * features, bytes_accessed=2 * (depth + rows) * features, transcendentals=0
        ),
        name="input_step",
    )(place, cot, w_own, *w_rest)


def total_kernel(ours, theirs, mask, out):
    total = ours[...].astype(jnp.float32) + theirs[...].astype(jnp.float32)
    out[...] = (total * mask[...]).astype(jnp.bfloat16)


def total_step(ours, theirs, mask):
    rows, features = ours.shape
    spec = pl.BlockSpec((rows, features // 2), lambda i: (0, i))
    return pl.pallas_call(
        total_kernel,
        grid=(features // (features // 2),),
        in_specs=[spec, spec, pl.BlockSpec((rows, 1), lambda i: (0, 0))],
        out_specs=spec,
        out_shape=jax.ShapeDtypeStruct(ours.shape, jnp.bfloat16),
        compiler_params=params(),
        cost_estimate=COST,
        name="total_step",
    )(ours, theirs, mask)


def after(arrays, *others):
    return lax.optimization_barrier((arrays, *others))[0]


def per_device(tokens_in, key_cot, row_mask, w_key, momentum):
    position = lax.axis_index("tensor")
    chip, core = position // CORES, position % CORES
    y = lax.axis_index("dp") % YS
    inner = (chip == 1) | (chip == 2)
    features = w_key.shape[0]
    share = tokens_in.shape[0]
    quarter = features // YS
    cut = CUT
    prior = momentum[0]
    place = jnp.stack(
        [
            of_chip * CORES + of_core
            for of_chip in (chip, chip ^ 1, chip ^ 3, chip ^ 2)
            for of_core in (core, 1 - core)
        ]
    ).astype(jnp.int32)

    tokens = jnp.where(row_mask[:, None] != 0, tokens_in, jnp.zeros_like(tokens_in))
    tokens, w_first = lax.optimization_barrier((tokens, w_key))
    w_part = lax.dynamic_slice(w_first, (y * quarter, 0), (quarter, 128))
    near, side = across(tokens), inward(tokens)
    w_here = jnp.concatenate([in_pair(w_part), out_of_pair(w_part), opposite_heads(w_part)], 1)
    w_next, w_before = along_y(w_here, 1), along_y(w_here, -1)
    cot_pieces = [
        lax.dynamic_slice(key_cot, ((chip ^ step) * CORES * share, 0), (CORES * share, 128))
        for step in (0, 1, 3, 2)
    ]
    near, side, w_next, w_before, key_cot, cot_pieces, lend = lax.optimization_barrier(
        (near, side, w_next, w_before, key_cot, cot_pieces, [prior[:cut], prior[cut:]])
    )

    far = across(side[:, :cut])
    cot_side = inward(key_cot)
    lent = inward(lend[0])
    own_swapped, near_swapped, side_swapped = core_swap(tokens), core_swap(near), core_swap(side)
    cot_pieces, own_swapped, near_swapped, side_swapped = lax.optimization_barrier(
        (cot_pieces, own_swapped, near_swapped, side_swapped)
    )
    for i, step in ((1, 1), (2, 3), (3, 2)):
        cot_pieces[i] = permute(cot_pieces[i], lambda h, y, c, k, step=step: (h, y, c ^ step, k))
    w_far = [w_next[: quarter // 2], w_before[quarter // 2 :]]
    arrays = (tokens, own_swapped, side, side_swapped, near, near_swapped)

    def early(start, size):
        return gather_step(place, [(array, start) for array in arrays], key_cot, (cot_side, 0), start, size)

    summed = [early(0, cut), early(cut, features - cut)]
    far, lent, summed, cot_pieces, w_far, side = lax.optimization_barrier(
        (far, lent, summed, cot_pieces, w_far, side)
    )

    far_late = across(side[:, cut:])
    lent_late = inward(lend[1])
    new_own, new_side, words, side_words = momentum_step(
        place, far, core_swap(far), key_cot, (cot_side, 0), summed[0], prior, lent, 0, []
    )
    returned = outward(new_side)
    w_far = [along_y(w_far[0], 1), along_y(w_far[1], -1)]
    w_other = core_swap(w_key)
    cot_mine = jnp.concatenate(cot_pieces, 1)
    theirs = lax.dynamic_slice(cot_mine, ((1 - core) * share, 0), (share, 512))
    ours = lax.dynamic_slice(cot_mine, (core * share, 0), (share, 512))
    cot_mine = jnp.concatenate([ours, theirs], 0)
    far_late, lent_late, returned, new_own, words, side_words, cot_mine, w_other = lax.optimization_barrier(
        (far_late, lent_late, returned, new_own, words, side_words, cot_mine, w_other)
    )

    new_own, new_side, words, side_words = momentum_step(
        place, far_late, core_swap(far_late), key_cot, (cot_side, 0), summed[1], prior, lent_late, cut,
        [new_own, words, side_words],
    )
    is_inner = inner.astype(jnp.int32)[None]
    words, side_words, cot_mine = lax.optimization_barrier((words, side_words, cot_mine))
    words = jnp.where(inner, words, outward(side_words))
    pair = jnp.stack([words, z_flip(words)])
    quarters = jnp.stack([y, (y + 1) % YS, (y + 3) % YS, (y + 2) % YS]).astype(jnp.int32)
    ours, theirs = input_step(quarters, cot_mine, w_key, [w_here, w_next, w_before, *w_far])
    pair, new_side, ours, theirs = lax.optimization_barrier((pair, new_side, ours, theirs))

    votes = [pair, along_y(pair, 1), along_y(pair, -1), along_y(pair, 2)]
    returned_late = outward(new_side)
    input_grad = total_step(ours, core_swap(theirs), row_mask.astype(jnp.float32)[:, None])
    new_own = choose_step(is_inner, new_own, returned, 0)
    votes_other = [core_swap(piece) for piece in votes]
    rollout_weight = vote_step(core[None], votes, votes_other, w_key, w_other)[None]
    new_momentum = choose_step(is_inner, new_own, returned_late, cut)[None]
    return (input_grad, new_momentum, rollout_weight)


def solution(mesh):
    return jax.shard_map(
        per_device,
        mesh=mesh,
        in_specs=(
            P(("section", "dp", "tensor"), None),
            P(("section", "dp"), "tensor"),
            P(("section", "dp", "tensor")),
            P("section", "tensor"),
            P("dp", "section", "tensor"),
        ),
        out_specs=(
            P(("section", "dp", "tensor"), None),
            P("dp", "section", "tensor"),
            P("tensor", "section", None),
        ),
        check_vma=False,
    )
```

```python
import jax
import jax.numpy as jnp
from jax import lax
from jax.experimental import pallas as pl
from jax.experimental.pallas import tpu as pltpu
from jax.sharding import PartitionSpec as P

beta_slow = 0.99
beta_vote = 0.9
step_rate = 0.02

AXES = ("dp", "tensor")
HI, YS, LINE, CORES = 2, 4, 4, 2
WIDTH = 1024
PACK = 512
CUT = 2048
COST = pl.CostEstimate(flops=2_000_000_000, bytes_accessed=10_000_000, transcendentals=0)
VMEM = 48 * 1024 * 1024


def permute(array, place):
    pairs = []
    for hi in range(HI):
        for y in range(YS):
            for c in range(LINE):
                for k in range(CORES):
                    to = place(hi, y, c, k)
                    if to is not None:
                        h2, y2, c2, k2 = to
                        source = ((hi * YS + y) * LINE + c) * CORES + k
                        target = ((h2 % HI * YS + y2 % YS) * LINE + c2) * CORES + k2
                        pairs.append((source, target))
    return lax.ppermute(array, AXES, pairs)


def core_swap(array):
    return permute(array, lambda h, y, c, k: (h, y, c, 1 - k))


def along_y(array, step):
    return permute(array, lambda h, y, c, k: (h, y - step, c, k))


def in_pair(array):
    return permute(array, lambda h, y, c, k: (h, y, c ^ 1, k))


def out_of_pair(array):
    def place(h, y, c, k):
        z = (h * LINE + c + (1 if c % 2 else -1)) % (HI * LINE)
        return z // LINE, y, z % LINE, k

    return permute(array, place)


def opposite_heads(array):
    def place(h, y, c, k):
        z = (h * LINE + c + (2 if c >= 2 else -2)) % (HI * LINE)
        return z // LINE, y, z % LINE, k

    return permute(array, place)


def inward(array):
    return permute(array, lambda h, y, c, k: (h, y, c ^ 1, k) if c in (0, 3) else None)


def outward(array):
    return permute(array, lambda h, y, c, k: (h, y, c ^ 1, k) if c in (1, 2) else None)


def across(array):
    return permute(array, lambda h, y, c, k: (h, y, 3 - c, k) if c in (1, 2) else None)


def z_flip(array):
    return permute(array, lambda h, y, c, k: (h ^ 1, y, c, k))


def params():
    return pltpu.CompilerParams(vmem_limit_bytes=VMEM)


def cot_rows(place, first, count, cot_own, cot_side):
    share = cot_own.shape[0] // (LINE * CORES)
    blocks = [pl.ds(pl.multiple_of(place[first + i] * share, share), share) for i in range(count)]
    return jnp.concatenate(
        [jnp.concatenate([ref[block, :] for block in blocks], 0) for ref in (cot_own, cot_side)], 1
    )


def multiply(tokens, cot):
    rows = jnp.concatenate([ref[...] for ref in tokens], 0)
    return lax.dot_general(rows, cot, (((0,), (0,)), ((), ())), preferred_element_type=jnp.float32)


def gather_kernel(place, *refs):
    tokens, cot_own, cot_side, out, cot = refs[:-4], refs[-4], refs[-3], refs[-2], refs[-1]

    @pl.when(pl.program_id(0) == 0)
    def _():
        cot[...] = cot_rows(place, 0, len(tokens), cot_own, cot_side)

    out[...] = multiply(tokens, cot[...])


def gather_step(place, tokens, cot_own, cot_side, start, size):
    share, rows = tokens[0][0].shape[0], cot_own.shape[0]
    return pl.pallas_call(
        gather_kernel,
        grid_spec=pltpu.PrefetchScalarGridSpec(
            num_scalar_prefetch=1,
            grid=(size // WIDTH,),
            in_specs=[
                pl.BlockSpec((share, WIDTH), lambda i, place, skip=first // WIDTH: (0, i + skip))
                for _, first in tokens
            ]
            + [
                pl.BlockSpec((rows, 128), lambda i, place: (0, 0)),
                pl.BlockSpec((rows, 128), lambda i, place: (cot_side[1], 0)),
            ],
            out_specs=pl.BlockSpec((WIDTH, 256), lambda i, place: (i, 0)),
            scratch_shapes=[pltpu.VMEM((len(tokens) * share, 256), jnp.bfloat16)],
        ),
        out_shape=jax.ShapeDtypeStruct((size, 256), jnp.float32),
        compiler_params=params(),
        cost_estimate=COST,
        name="gather_step",
    )(place, *[array for array, _ in tokens], cot_own, cot_side[0])


def momentum_kernel(place, *refs):
    first, second, cot_own, cot_side, early, prior_own, prior_side = refs[:7]
    new_own, new_side, words_own, words_side = refs[-4:]
    grad = early[...] + multiply((first, second), cot_rows(place, 6, 2, cot_own, cot_side))
    for i, (prior, new, words) in enumerate(
        ((prior_own, new_own, words_own), (prior_side, new_side, words_side))
    ):
        part = grad[:, i * 128 : (i + 1) * 128]
        before = prior[...].astype(jnp.float32)
        new[...] = (beta_slow * before + (1.0 - beta_slow) * part).astype(jnp.bfloat16)
        positive = (beta_vote * before + (1.0 - beta_vote) * part > 0).astype(jnp.int32)
        step = PACK // 32
        for block in range(WIDTH // PACK):
            start = block * PACK
            packed = positive[start : start + step]
            for bit in range(1, 32):
                packed = packed | (positive[start + bit * step : start + (bit + 1) * step] << bit)
            words[block * step : (block + 1) * step, :] = packed


def momentum_step(place, first, second, cot_own, cot_side, early, prior_own, prior_side, start, buffers):
    share, size = first.shape
    rows = cot_own.shape[0]
    features = prior_own.shape[0]
    skip = start // WIDTH
    here = lambda i, place: (i, 0)
    there = lambda i, place: (i + skip, 0)
    token_spec = pl.BlockSpec((share, WIDTH), lambda i, place: (0, i))
    word_spec = pl.BlockSpec((WIDTH // 32, 128), there)
    word_shape = jax.ShapeDtypeStruct((features // 32, 128), jnp.int32)
    return pl.pallas_call(
        momentum_kernel,
        grid_spec=pltpu.PrefetchScalarGridSpec(
            num_scalar_prefetch=1,
            grid=(size // WIDTH,),
            in_specs=[
                token_spec,
                token_spec,
                pl.BlockSpec((rows, 128), lambda i, place: (0, 0)),
                pl.BlockSpec((rows, 128), lambda i, place: (cot_side[1], 0)),
                pl.BlockSpec((WIDTH, 256), here),
                pl.BlockSpec((WIDTH, 128), there),
                pl.BlockSpec((WIDTH, 128), here),
            ]
            + [pl.BlockSpec(memory_space=pl.ANY)] * len(buffers),
            out_specs=[
                pl.BlockSpec((WIDTH, 128), there),
                pl.BlockSpec((WIDTH, 128), here),
                word_spec,
                word_spec,
            ],
        ),
        out_shape=[
            jax.ShapeDtypeStruct((features, 128), jnp.bfloat16),
            jax.ShapeDtypeStruct((size, 128), jnp.bfloat16),
            word_shape,
            word_shape,
        ],
        input_output_aliases={8: 0, 9: 2, 10: 3} if buffers else {},
        compiler_params=params(),
        cost_estimate=COST,
        name="momentum_step",
    )(place, first, second, cot_own, cot_side[0], early, prior_own, prior_side, *buffers)


def majority(words):
    def half(a, b):
        return a ^ b, a & b

    def full(a, b, c):
        x = a ^ b
        return x ^ c, (a & b) | (x & c)

    s0, c0 = full(words[0], words[1], words[2])
    s1, c1 = full(words[3], words[4], words[5])
    s2, c2 = half(words[6], words[7])
    ones, c3 = full(s0, s1, s2)
    t0, d0 = full(c0, c1, c2)
    twos, d1 = half(t0, c3)
    fours, eights = half(d0, d1)
    more = eights | (fours & (ones | twos))
    fewer = ~(eights | fours)
    return more, fewer


def fill_kernel(inner, low, high, own, out, sems):
    @pl.when(inner[0] == 0)
    def _():
        copies = [
            pltpu.make_async_copy(ref, out.at[pl.ds(start, ref.shape[0])], sems.at[i])
            for i, (ref, start) in enumerate(((low, 0), (high, low.shape[0])))
        ]
        for copy in copies:
            copy.start()
        for copy in copies:
            copy.wait()


def fill_step(inner, low, high, own):
    anywhere = pl.BlockSpec(memory_space=pl.ANY)
    return pl.pallas_call(
        fill_kernel,
        grid_spec=pltpu.PrefetchScalarGridSpec(
            num_scalar_prefetch=1,
            grid=(1,),
            in_specs=[anywhere] * 3,
            out_specs=anywhere,
            scratch_shapes=[pltpu.SemaphoreType.DMA((2,))],
        ),
        out_shape=jax.ShapeDtypeStruct(own.shape, own.dtype),
        input_output_aliases={3: 0},
        compiler_params=params(),
        cost_estimate=COST,
        name="fill_step",
    )(inner, low, high, own)


def vote_kernel(core, *refs):
    words_own, words_other, (w_own, w_other, out) = refs[:4], refs[4:8], refs[8:]
    is_low = core[0] == 0
    step = PACK // 32
    for block in range(out.shape[0] // PACK):
        rows = slice(block * PACK, (block + 1) * PACK)
        updated = []
        for words, weights in ((words_own, w_own), (words_other, w_other)):
            more, fewer = majority(
                [ref[i, block * step : (block + 1) * step] for ref in words for i in range(2)]
            )
            direction = jnp.concatenate(
                [((more >> bit) & 1) - ((fewer >> bit) & 1) for bit in range(32)], 0
            ).astype(jnp.float32)
            updated.append(
                (weights[rows, :].astype(jnp.float32) - step_rate * direction).astype(jnp.bfloat16)
            )
        out[rows, :128] = jnp.where(is_low, updated[0], updated[1])
        out[rows, 128:] = jnp.where(is_low, updated[1], updated[0])


def vote_step(core, words_own, words_other, w_own, w_other):
    features = w_own.shape[0]
    size = features // 2
    word_spec = pl.BlockSpec((2, size // 32, 128), lambda i, core: (0, i, 0))
    weight_spec = pl.BlockSpec((size, 128), lambda i, core: (i, 0))
    return pl.pallas_call(
        vote_kernel,
        grid_spec=pltpu.PrefetchScalarGridSpec(
            num_scalar_prefetch=1,
            grid=(features // size,),
            in_specs=[word_spec] * 8 + [weight_spec] * 2,
            out_specs=pl.BlockSpec((size, 256), lambda i, core: (i, 0)),
        ),
        out_shape=jax.ShapeDtypeStruct((features, 256), jnp.bfloat16),
        compiler_params=params(),
        cost_estimate=COST,
        name="vote_step",
    )(core, *words_own, *words_other, w_own, w_other)


def input_kernel(place, cot, w_own, here, following, before, far_low, far_high, ours, theirs):
    rows = ours.shape[0]

    def product(w_rest):
        weights = jnp.concatenate([w_own[...], w_rest], 1)
        total = lax.dot_general(
            cot[...], weights, (((1,), (1,)), ((), ())), preferred_element_type=jnp.float32
        ).astype(jnp.bfloat16)
        ours[...] = total[:rows]
        theirs[...] = total[rows:]

    i = pl.program_id(0)
    for at, ref in enumerate((here, following, before)):
        pl.when(i == at)(lambda ref=ref: product(ref[...]))
    pl.when(i == 3)(lambda: product(jnp.concatenate([far_low[...], far_high[...]], 0)))


def input_step(place, cot, w_own, w_rest):
    rows, depth = cot.shape
    features = w_own.shape[0]
    width = features // YS
    out_spec = pl.BlockSpec((rows // 2, width), lambda i, place: (0, place[i]))
    return pl.pallas_call(
        input_kernel,
        grid_spec=pltpu.PrefetchScalarGridSpec(
            num_scalar_prefetch=1,
            grid=(YS,),
            in_specs=[
                pl.BlockSpec((rows, depth), lambda i, place: (0, 0)),
                pl.BlockSpec((width, 128), lambda i, place: (place[i], 0)),
            ]
            + [pl.BlockSpec(w.shape, lambda i, place: (0, 0)) for w in w_rest],
            out_specs=[out_spec] * 2,
        ),
        out_shape=[jax.ShapeDtypeStruct((rows // 2, features), jnp.bfloat16)] * 2,
        compiler_params=params(),
        cost_estimate=pl.CostEstimate(
            flops=2 * rows * depth * features, bytes_accessed=2 * (depth + rows) * features, transcendentals=0
        ),
        name="input_step",
    )(place, cot, w_own, *w_rest)


def total_kernel(ours, theirs, mask, out):
    total = ours[...].astype(jnp.float32) + theirs[...].astype(jnp.float32)
    out[...] = (total * mask[...]).astype(jnp.bfloat16)


def total_step(ours, theirs, mask):
    rows, features = ours.shape
    spec = pl.BlockSpec((rows, features // 2), lambda i: (0, i))
    return pl.pallas_call(
        total_kernel,
        grid=(features // (features // 2),),
        in_specs=[spec, spec, pl.BlockSpec((rows, 1), lambda i: (0, 0))],
        out_specs=spec,
        out_shape=jax.ShapeDtypeStruct(ours.shape, jnp.bfloat16),
        compiler_params=params(),
        cost_estimate=COST,
        name="total_step",
    )(ours, theirs, mask)


def after(arrays, *others):
    return lax.optimization_barrier((arrays, *others))[0]


def per_device(tokens_in, key_cot, row_mask, w_key, momentum):
    position = lax.axis_index("tensor")
    chip, core = position // CORES, position % CORES
    y = lax.axis_index("dp") % YS
    inner = (chip == 1) | (chip == 2)
    features = w_key.shape[0]
    share = tokens_in.shape[0]
    quarter = features // YS
    cut = CUT
    prior = momentum[0]
    place = jnp.stack(
        [
            of_chip * CORES + of_core
            for of_chip in (chip, chip ^ 1, chip ^ 3, chip ^ 2)
            for of_core in (core, 1 - core)
        ]
    ).astype(jnp.int32)

    tokens = jnp.where(row_mask[:, None] != 0, tokens_in, jnp.zeros_like(tokens_in))
    tokens, w_first = lax.optimization_barrier((tokens, w_key))
    w_part = lax.dynamic_slice(w_first, (y * quarter, 0), (quarter, 128))
    near, side = across(tokens), inward(tokens)
    w_here = jnp.concatenate([in_pair(w_part), out_of_pair(w_part), opposite_heads(w_part)], 1)
    w_next, w_before = along_y(w_here, 1), along_y(w_here, -1)
    cot_pieces = [
        lax.dynamic_slice(key_cot, ((chip ^ step) * CORES * share, 0), (CORES * share, 128))
        for step in (0, 1, 3, 2)
    ]
    near, side, w_next, w_before, key_cot, cot_pieces, lend = lax.optimization_barrier(
        (near, side, w_next, w_before, key_cot, cot_pieces, [prior[:cut], prior[cut:]])
    )

    far = across(side[:, :cut])
    cot_side = inward(key_cot)
    lent = inward(lend[0])
    own_swapped, near_swapped, side_swapped = core_swap(tokens), core_swap(near), core_swap(side)
    cot_pieces, own_swapped, near_swapped, side_swapped = lax.optimization_barrier(
        (cot_pieces, own_swapped, near_swapped, side_swapped)
    )
    for i, step in ((1, 1), (2, 3), (3, 2)):
        cot_pieces[i] = permute(cot_pieces[i], lambda h, y, c, k, step=step: (h, y, c ^ step, k))
    w_far = [w_next[: quarter // 2], w_before[quarter // 2 :]]
    arrays = (tokens, own_swapped, side, side_swapped, near, near_swapped)

    def early(start, size):
        return gather_step(place, [(array, start) for array in arrays], key_cot, (cot_side, 0), start, size)

    summed = [early(0, cut), early(cut, features - cut)]
    far, lent, summed, cot_pieces, w_far, side = lax.optimization_barrier(
        (far, lent, summed, cot_pieces, w_far, side)
    )

    far_late = across(side[:, cut:])
    lent_late = inward(lend[1])
    new_own, new_side, words, side_words = momentum_step(
        place, far, core_swap(far), key_cot, (cot_side, 0), summed[0], prior, lent, 0, []
    )
    returned = outward(new_side)
    w_far = [along_y(w_far[0], 1), along_y(w_far[1], -1)]
    w_other = core_swap(w_key)
    cot_mine = jnp.concatenate(cot_pieces, 1)
    theirs = lax.dynamic_slice(cot_mine, ((1 - core) * share, 0), (share, 512))
    ours = lax.dynamic_slice(cot_mine, (core * share, 0), (share, 512))
    cot_mine = jnp.concatenate([ours, theirs], 0)
    far_late, lent_late, returned, new_own, words, side_words, cot_mine, w_other = lax.optimization_barrier(
        (far_late, lent_late, returned, new_own, words, side_words, cot_mine, w_other)
    )

    new_own, new_side, words, side_words = momentum_step(
        place, far_late, core_swap(far_late), key_cot, (cot_side, 0), summed[1], prior, lent_late, cut,
        [new_own, words, side_words],
    )
    is_inner = inner.astype(jnp.int32)[None]
    words, side_words, cot_mine = lax.optimization_barrier((words, side_words, cot_mine))
    words = jnp.where(inner, words, outward(side_words))
    pair = jnp.stack([words, z_flip(words)])
    quarters = jnp.stack([y, (y + 1) % YS, (y + 3) % YS, (y + 2) % YS]).astype(jnp.int32)
    ours, theirs = input_step(quarters, cot_mine, w_key, [w_here, w_next, w_before, *w_far])
    pair, new_side, ours, theirs = lax.optimization_barrier((pair, new_side, ours, theirs))

    votes = [pair, along_y(pair, 1), along_y(pair, -1), along_y(pair, 2)]
    returned_late = outward(new_side)
    input_grad = total_step(ours, core_swap(theirs), row_mask.astype(jnp.float32)[:, None])
    votes, input_grad = lax.optimization_barrier((votes, input_grad))
    votes_other = [core_swap(piece) for piece in votes]
    rollout_weight = vote_step(core[None], votes, votes_other, w_key, w_other)
    returned_late, rollout_weight = lax.optimization_barrier((returned_late, rollout_weight))
    new_momentum = fill_step(is_inner, returned, returned_late, new_own)
    return (input_grad, new_momentum[None], rollout_weight[None])


def solution(mesh):
    return jax.shard_map(
        per_device,
        mesh=mesh,
        in_specs=(
            P(("section", "dp", "tensor"), None),
            P(("section", "dp"), "tensor"),
            P(("section", "dp", "tensor")),
            P("section", "tensor"),
            P("dp", "section", "tensor"),
        ),
        out_specs=(
            P(("section", "dp", "tensor"), None),
            P("dp", "section", "tensor"),
            P("tensor", "section", None),
        ),
        check_vma=False,
    )
```

```python
import jax
import jax.numpy as jnp
from jax import lax
from jax.experimental import pallas as pl
from jax.experimental.pallas import tpu as pltpu
from jax.sharding import PartitionSpec as P

beta_slow = 0.99
beta_vote = 0.9
step_rate = 0.02

AXES = ("dp", "tensor")
HI, YS, LINE, CORES = 2, 4, 4, 2
WIDTH = 1024
PACK = 512
CUT = 2048
COST = pl.CostEstimate(flops=2_000_000_000, bytes_accessed=10_000_000, transcendentals=0)
VMEM = 48 * 1024 * 1024


def permute(array, place):
    pairs = []
    for hi in range(HI):
        for y in range(YS):
            for c in range(LINE):
                for k in range(CORES):
                    to = place(hi, y, c, k)
                    if to is not None:
                        h2, y2, c2, k2 = to
                        source = ((hi * YS + y) * LINE + c) * CORES + k
                        target = ((h2 % HI * YS + y2 % YS) * LINE + c2) * CORES + k2
                        pairs.append((source, target))
    return lax.ppermute(array, AXES, pairs)


def core_swap(array):
    return permute(array, lambda h, y, c, k: (h, y, c, 1 - k))


def along_y(array, step):
    return permute(array, lambda h, y, c, k: (h, y - step, c, k))


def in_pair(array):
    return permute(array, lambda h, y, c, k: (h, y, c ^ 1, k))


def out_of_pair(array):
    def place(h, y, c, k):
        z = (h * LINE + c + (1 if c % 2 else -1)) % (HI * LINE)
        return z // LINE, y, z % LINE, k

    return permute(array, place)


def opposite_heads(array):
    def place(h, y, c, k):
        z = (h * LINE + c + (2 if c >= 2 else -2)) % (HI * LINE)
        return z // LINE, y, z % LINE, k

    return permute(array, place)


def inward(array):
    return permute(array, lambda h, y, c, k: (h, y, c ^ 1, k) if c in (0, 3) else None)


def outward(array):
    return permute(array, lambda h, y, c, k: (h, y, c ^ 1, k) if c in (1, 2) else None)


def across(array):
    return permute(array, lambda h, y, c, k: (h, y, 3 - c, k) if c in (1, 2) else None)


def z_flip(array):
    return permute(array, lambda h, y, c, k: (h ^ 1, y, c, k))


def params():
    return pltpu.CompilerParams(vmem_limit_bytes=VMEM)


def cot_rows(place, first, count, cot_own, cot_side):
    share = cot_own.shape[0] // (LINE * CORES)
    blocks = [pl.ds(pl.multiple_of(place[first + i] * share, share), share) for i in range(count)]
    return jnp.concatenate(
        [jnp.concatenate([ref[block, :] for block in blocks], 0) for ref in (cot_own, cot_side)], 1
    )


def multiply(tokens, cot):
    rows = jnp.concatenate([ref[...] for ref in tokens], 0)
    return lax.dot_general(rows, cot, (((0,), (0,)), ((), ())), preferred_element_type=jnp.float32)


def gather_kernel(place, *refs):
    tokens, cot_own, cot_side, out, cot = refs[:-4], refs[-4], refs[-3], refs[-2], refs[-1]

    @pl.when(pl.program_id(0) == 0)
    def _():
        cot[...] = cot_rows(place, 0, len(tokens), cot_own, cot_side)

    out[...] = multiply(tokens, cot[...])


def gather_step(place, tokens, cot_own, cot_side, start, size):
    share, rows = tokens[0][0].shape[0], cot_own.shape[0]
    return pl.pallas_call(
        gather_kernel,
        grid_spec=pltpu.PrefetchScalarGridSpec(
            num_scalar_prefetch=1,
            grid=(size // WIDTH,),
            in_specs=[
                pl.BlockSpec((share, WIDTH), lambda i, place, skip=first // WIDTH: (0, i + skip))
                for _, first in tokens
            ]
            + [
                pl.BlockSpec((rows, 128), lambda i, place: (0, 0)),
                pl.BlockSpec((rows, 128), lambda i, place: (cot_side[1], 0)),
            ],
            out_specs=pl.BlockSpec((WIDTH, 256), lambda i, place: (i, 0)),
            scratch_shapes=[pltpu.VMEM((len(tokens) * share, 256), jnp.bfloat16)],
        ),
        out_shape=jax.ShapeDtypeStruct((size, 256), jnp.float32),
        compiler_params=params(),
        cost_estimate=COST,
        name="gather_step",
    )(place, *[array for array, _ in tokens], cot_own, cot_side[0])


def momentum_kernel(place, *refs):
    first, second, cot_own, cot_side, early, prior_own, prior_side = refs[:7]
    new_own, new_side, words_own, words_side, cot = refs[-5:]

    @pl.when(pl.program_id(0) == 0)
    def _():
        cot[...] = cot_rows(place, 6, 2, cot_own, cot_side)

    grad = early[...] + multiply((first, second), cot[...])
    for i, (prior, new, words) in enumerate(
        ((prior_own, new_own, words_own), (prior_side, new_side, words_side))
    ):
        part = grad[:, i * 128 : (i + 1) * 128]
        before = prior[...].astype(jnp.float32)
        new[...] = (beta_slow * before + (1.0 - beta_slow) * part).astype(jnp.bfloat16)
        positive = (beta_vote * before + (1.0 - beta_vote) * part > 0).astype(jnp.int32)
        step = PACK // 32
        for block in range(WIDTH // PACK):
            start = block * PACK
            packed = positive[start : start + step]
            for bit in range(1, 32):
                packed = packed | (positive[start + bit * step : start + (bit + 1) * step] << bit)
            words[block * step : (block + 1) * step, :] = packed


def momentum_step(place, first, second, cot_own, cot_side, early, prior_own, prior_side, start, buffers):
    share, size = first.shape
    rows = cot_own.shape[0]
    features = prior_own.shape[0]
    skip = start // WIDTH
    here = lambda i, place: (i, 0)
    there = lambda i, place: (i + skip, 0)
    token_spec = pl.BlockSpec((share, WIDTH), lambda i, place: (0, i))
    word_spec = pl.BlockSpec((WIDTH // 32, 128), there)
    word_shape = jax.ShapeDtypeStruct((features // 32, 128), jnp.int32)
    return pl.pallas_call(
        momentum_kernel,
        grid_spec=pltpu.PrefetchScalarGridSpec(
            num_scalar_prefetch=1,
            grid=(size // WIDTH,),
            in_specs=[
                token_spec,
                token_spec,
                pl.BlockSpec((rows, 128), lambda i, place: (0, 0)),
                pl.BlockSpec((rows, 128), lambda i, place: (cot_side[1], 0)),
                pl.BlockSpec((WIDTH, 256), here),
                pl.BlockSpec((WIDTH, 128), there),
                pl.BlockSpec((WIDTH, 128), here),
            ]
            + [pl.BlockSpec(memory_space=pl.ANY)] * len(buffers),
            out_specs=[
                pl.BlockSpec((WIDTH, 128), there),
                pl.BlockSpec((WIDTH, 128), here),
                word_spec,
                word_spec,
            ],
            scratch_shapes=[pltpu.VMEM((2 * share, 256), jnp.bfloat16)],
        ),
        out_shape=[
            jax.ShapeDtypeStruct((features, 128), jnp.bfloat16),
            jax.ShapeDtypeStruct((size, 128), jnp.bfloat16),
            word_shape,
            word_shape,
        ],
        input_output_aliases={8: 0, 9: 2, 10: 3} if buffers else {},
        compiler_params=params(),
        cost_estimate=COST,
        name="momentum_step",
    )(place, first, second, cot_own, cot_side[0], early, prior_own, prior_side, *buffers)


def majority(words):
    def half(a, b):
        return a ^ b, a & b

    def full(a, b, c):
        x = a ^ b
        return x ^ c, (a & b) | (x & c)

    s0, c0 = full(words[0], words[1], words[2])
    s1, c1 = full(words[3], words[4], words[5])
    s2, c2 = half(words[6], words[7])
    ones, c3 = full(s0, s1, s2)
    t0, d0 = full(c0, c1, c2)
    twos, d1 = half(t0, c3)
    fours, eights = half(d0, d1)
    more = eights | (fours & (ones | twos))
    fewer = ~(eights | fours)
    return more, fewer


def fill_kernel(inner, low, high, own, out, sems):
    @pl.when(inner[0] == 0)
    def _():
        copies = [
            pltpu.make_async_copy(ref, out.at[pl.ds(start, ref.shape[0])], sems.at[i])
            for i, (ref, start) in enumerate(((low, 0), (high, low.shape[0])))
        ]
        for copy in copies:
            copy.start()
        for copy in copies:
            copy.wait()


def fill_step(inner, low, high, own):
    anywhere = pl.BlockSpec(memory_space=pl.ANY)
    return pl.pallas_call(
        fill_kernel,
        grid_spec=pltpu.PrefetchScalarGridSpec(
            num_scalar_prefetch=1,
            grid=(1,),
            in_specs=[anywhere] * 3,
            out_specs=anywhere,
            scratch_shapes=[pltpu.SemaphoreType.DMA((2,))],
        ),
        out_shape=jax.ShapeDtypeStruct(own.shape, own.dtype),
        input_output_aliases={3: 0},
        compiler_params=params(),
        cost_estimate=COST,
        name="fill_step",
    )(inner, low, high, own)


def vote_kernel(core, *refs):
    words_own, words_other, (w_own, w_other, out) = refs[:4], refs[4:8], refs[8:]
    is_low = core[0] == 0
    step = PACK // 32
    for block in range(out.shape[0] // PACK):
        rows = slice(block * PACK, (block + 1) * PACK)
        updated = []
        for words, weights in ((words_own, w_own), (words_other, w_other)):
            more, fewer = majority(
                [ref[i, block * step : (block + 1) * step] for ref in words for i in range(2)]
            )
            direction = jnp.concatenate(
                [((more >> bit) & 1) - ((fewer >> bit) & 1) for bit in range(32)], 0
            ).astype(jnp.float32)
            updated.append(
                (weights[rows, :].astype(jnp.float32) - step_rate * direction).astype(jnp.bfloat16)
            )
        out[rows, :128] = jnp.where(is_low, updated[0], updated[1])
        out[rows, 128:] = jnp.where(is_low, updated[1], updated[0])


def vote_step(core, words_own, words_other, w_own, w_other):
    features = w_own.shape[0]
    size = features // 2
    word_spec = pl.BlockSpec((2, size // 32, 128), lambda i, core: (0, i, 0))
    weight_spec = pl.BlockSpec((size, 128), lambda i, core: (i, 0))
    return pl.pallas_call(
        vote_kernel,
        grid_spec=pltpu.PrefetchScalarGridSpec(
            num_scalar_prefetch=1,
            grid=(features // size,),
            in_specs=[word_spec] * 8 + [weight_spec] * 2,
            out_specs=pl.BlockSpec((size, 256), lambda i, core: (i, 0)),
        ),
        out_shape=jax.ShapeDtypeStruct((features, 256), jnp.bfloat16),
        compiler_params=params(),
        cost_estimate=COST,
        name="vote_step",
    )(core, *words_own, *words_other, w_own, w_other)


def input_kernel(place, cot, w_own, here, following, before, far_low, far_high, ours, theirs):
    rows = ours.shape[0]

    def product(w_rest):
        weights = jnp.concatenate([w_own[...], w_rest], 1)
        total = lax.dot_general(
            cot[...], weights, (((1,), (1,)), ((), ())), preferred_element_type=jnp.float32
        ).astype(jnp.bfloat16)
        ours[...] = total[:rows]
        theirs[...] = total[rows:]

    i = pl.program_id(0)
    for at, ref in enumerate((here, following, before)):
        pl.when(i == at)(lambda ref=ref: product(ref[...]))
    pl.when(i == 3)(lambda: product(jnp.concatenate([far_low[...], far_high[...]], 0)))


def input_step(place, cot, w_own, w_rest):
    rows, depth = cot.shape
    features = w_own.shape[0]
    width = features // YS
    out_spec = pl.BlockSpec((rows // 2, width), lambda i, place: (0, place[i]))
    return pl.pallas_call(
        input_kernel,
        grid_spec=pltpu.PrefetchScalarGridSpec(
            num_scalar_prefetch=1,
            grid=(YS,),
            in_specs=[
                pl.BlockSpec((rows, depth), lambda i, place: (0, 0)),
                pl.BlockSpec((width, 128), lambda i, place: (place[i], 0)),
            ]
            + [pl.BlockSpec(w.shape, lambda i, place: (0, 0)) for w in w_rest],
            out_specs=[out_spec] * 2,
        ),
        out_shape=[jax.ShapeDtypeStruct((rows // 2, features), jnp.bfloat16)] * 2,
        compiler_params=params(),
        cost_estimate=pl.CostEstimate(
            flops=2 * rows * depth * features, bytes_accessed=2 * (depth + rows) * features, transcendentals=0
        ),
        name="input_step",
    )(place, cot, w_own, *w_rest)


def total_kernel(ours, theirs, mask, out):
    total = ours[...].astype(jnp.float32) + theirs[...].astype(jnp.float32)
    out[...] = (total * mask[...]).astype(jnp.bfloat16)


def total_step(ours, theirs, mask):
    rows, features = ours.shape
    spec = pl.BlockSpec((rows, features // 2), lambda i: (0, i))
    return pl.pallas_call(
        total_kernel,
        grid=(features // (features // 2),),
        in_specs=[spec, spec, pl.BlockSpec((rows, 1), lambda i: (0, 0))],
        out_specs=spec,
        out_shape=jax.ShapeDtypeStruct(ours.shape, jnp.bfloat16),
        compiler_params=params(),
        cost_estimate=COST,
        name="total_step",
    )(ours, theirs, mask)


def after(arrays, *others):
    return lax.optimization_barrier((arrays, *others))[0]


def per_device(tokens_in, key_cot, row_mask, w_key, momentum):
    position = lax.axis_index("tensor")
    chip, core = position // CORES, position % CORES
    y = lax.axis_index("dp") % YS
    inner = (chip == 1) | (chip == 2)
    features = w_key.shape[0]
    share = tokens_in.shape[0]
    quarter = features // YS
    cut = CUT
    prior = momentum[0]
    place = jnp.stack(
        [
            of_chip * CORES + of_core
            for of_chip in (chip, chip ^ 1, chip ^ 3, chip ^ 2)
            for of_core in (core, 1 - core)
        ]
    ).astype(jnp.int32)

    tokens = jnp.where(row_mask[:, None] != 0, tokens_in, jnp.zeros_like(tokens_in))
    tokens, w_first = lax.optimization_barrier((tokens, w_key))
    w_part = lax.dynamic_slice(w_first, (y * quarter, 0), (quarter, 128))
    near, side = across(tokens), inward(tokens)
    w_here = jnp.concatenate([in_pair(w_part), out_of_pair(w_part), opposite_heads(w_part)], 1)
    w_next, w_before = along_y(w_here, 1), along_y(w_here, -1)
    cot_pieces = [
        lax.dynamic_slice(key_cot, ((chip ^ step) * CORES * share, 0), (CORES * share, 128))
        for step in (0, 1, 3, 2)
    ]
    near, side, w_next, w_before, key_cot, cot_pieces, lend = lax.optimization_barrier(
        (near, side, w_next, w_before, key_cot, cot_pieces, [prior[:cut], prior[cut:]])
    )

    far = across(side[:, :cut])
    cot_side = inward(key_cot)
    lent = inward(lend[0])
    own_swapped, near_swapped, side_swapped = core_swap(tokens), core_swap(near), core_swap(side)
    cot_pieces, own_swapped, near_swapped, side_swapped = lax.optimization_barrier(
        (cot_pieces, own_swapped, near_swapped, side_swapped)
    )
    for i, step in ((1, 1), (2, 3), (3, 2)):
        cot_pieces[i] = permute(cot_pieces[i], lambda h, y, c, k, step=step: (h, y, c ^ step, k))
    w_far = [w_next[: quarter // 2], w_before[quarter // 2 :]]
    arrays = (tokens, own_swapped, side, side_swapped, near, near_swapped)

    def early(start, size):
        return gather_step(place, [(array, start) for array in arrays], key_cot, (cot_side, 0), start, size)

    summed = [early(0, cut), early(cut, features - cut)]
    far, lent, summed, cot_pieces, w_far, side = lax.optimization_barrier(
        (far, lent, summed, cot_pieces, w_far, side)
    )

    far_late = across(side[:, cut:])
    lent_late = inward(lend[1])
    new_own, new_side, words, side_words = momentum_step(
        place, far, core_swap(far), key_cot, (cot_side, 0), summed[0], prior, lent, 0, []
    )
    returned = outward(new_side)
    w_far = [along_y(w_far[0], 1), along_y(w_far[1], -1)]
    w_other = core_swap(w_key)
    cot_mine = jnp.concatenate(cot_pieces, 1)
    theirs = lax.dynamic_slice(cot_mine, ((1 - core) * share, 0), (share, 512))
    ours = lax.dynamic_slice(cot_mine, (core * share, 0), (share, 512))
    cot_mine = jnp.concatenate([ours, theirs], 0)
    far_late, lent_late, returned, new_own, words, side_words, cot_mine, w_other = lax.optimization_barrier(
        (far_late, lent_late, returned, new_own, words, side_words, cot_mine, w_other)
    )

    new_own, new_side, words, side_words = momentum_step(
        place, far_late, core_swap(far_late), key_cot, (cot_side, 0), summed[1], prior, lent_late, cut,
        [new_own, words, side_words],
    )
    is_inner = inner.astype(jnp.int32)[None]
    words, side_words, cot_mine = lax.optimization_barrier((words, side_words, cot_mine))
    words = jnp.where(inner, words, outward(side_words))
    pair = jnp.stack([words, z_flip(words)])
    quarters = jnp.stack([y, (y + 1) % YS, (y + 3) % YS, (y + 2) % YS]).astype(jnp.int32)
    ours, theirs = input_step(quarters, cot_mine, w_key, [w_here, w_next, w_before, *w_far])
    pair, new_side, ours, theirs = lax.optimization_barrier((pair, new_side, ours, theirs))

    votes = [pair, along_y(pair, 1), along_y(pair, -1), along_y(pair, 2)]
    returned_late = outward(new_side)
    input_grad = total_step(ours, core_swap(theirs), row_mask.astype(jnp.float32)[:, None])
    votes, input_grad = lax.optimization_barrier((votes, input_grad))
    votes_other = [core_swap(piece) for piece in votes]
    rollout_weight = vote_step(core[None], votes, votes_other, w_key, w_other)
    returned_late, rollout_weight = lax.optimization_barrier((returned_late, rollout_weight))
    new_momentum = fill_step(is_inner, returned, returned_late, new_own)
    return (input_grad, new_momentum[None], rollout_weight[None])


def solution(mesh):
    return jax.shard_map(
        per_device,
        mesh=mesh,
        in_specs=(
            P(("section", "dp", "tensor"), None),
            P(("section", "dp"), "tensor"),
            P(("section", "dp", "tensor")),
            P("section", "tensor"),
            P("dp", "section", "tensor"),
        ),
        out_specs=(
            P(("section", "dp", "tensor"), None),
            P("dp", "section", "tensor"),
            P("tensor", "section", None),
        ),
        check_vma=False,
    )
```
